32 devices in a mesh: groups: 2 (over y), lat: 4 (over z), row: 2 (over x), sub: 2 (over core).
Axes of the slice: x: 2, y: 2, z: 4, core: 2. Of those that a mesh axis runs over, the one named last changes fastest.
Arguments:
- target: bfloat16 [2048, 1536], P(('groups', 'lat', 'sub'), 'row'), parts along dimension 0, may hold values from -6 to 6
- dec_w: bfloat16 [16384, 1536], P(('groups', 'lat', 'sub'), 'row'), parts along dimension 0, may hold values from -0.4375 to 0.4375
- mom_first: bfloat16 [16384, 1536], P(('groups', 'lat', 'sub'), 'row'), parts along dimension 0, may hold values from -3 to 3
- mom_second: bfloat16 [16384, 1536], P(('groups', 'lat', 'sub'), 'row'), parts along dimension 0, may hold values from 0.0049743652 to 0.049804688
- ent_row: int32 [16, 2048], P(('groups', 'lat', 'sub')), parts along dimension 0, may hold values from 0 to 1023
- ent_lat: int32 [16, 2048], P(('groups', 'lat', 'sub')), parts along dimension 0, may hold values from 0 to 1023
- ent_val: bfloat16 [16, 2048], P(('groups', 'lat', 'sub')), parts along dimension 0, may hold values from 0 to 6, as said below
- block_count: int32 [16], P(('groups', 'lat', 'sub')), parts along dimension 0, may hold values from 1 to 16, as said below
Outputs:
- new_w: bfloat16 [16384, 1536], P(('groups', 'lat', 'sub'), 'row'), parts along dimension 0
- new_first: bfloat16 [16384, 1536], P(('groups', 'lat', 'sub'), 'row'), parts along dimension 0
- new_second: bfloat16 [16384, 1536], P(('groups', 'lat', 'sub'), 'row'), parts along dimension 0
The draws below stay inside these ranges and needn't reach their ends.
There are 2 independent parts, one for each index of `groups`. The reference program is written for one: setup_inputs(seed, part) draws one part's arguments, and reference() takes and returns one part's arrays. A program takes and returns all parts, laid end to end along the dimension named above; each array names one. Nothing has to cross between parts.
Inputs may be any that keep to these rules, and one draw needn't show every extreme that they name: `block_count`: at least one latent shard uses all 16 blocks. `ent_val`: slots j >= 128 * block_count[q] of shard q hold zero.
All inputs are finite; a program needn't handle non-finite values.
Results may differ from the reference program's by a relative error of at most 0.0057.
Values may be sent and summed in bfloat16 or wider, within the bound.
A program may use at most 64 MiB of HBM per device.

```python
import math
import jax
import jax.numpy as jnp
from jax import lax

DW = 1536
LAT_DEV = 1024
BLOCK = 128
MAXB = 16
ROWS = 1024
QS = 8
LATENTS = 8192


def shard_loads(key):
    shard_blocks = jax.random.randint(jax.random.fold_in(key, 101), (QS,), 1, MAXB)
    hottest = jax.random.randint(jax.random.fold_in(key, 102), (), 0, QS)
    shard_blocks = jnp.where(jnp.arange(QS) == hottest, MAXB, shard_blocks).astype(jnp.int32)
    shortfall = jax.random.randint(jax.random.fold_in(key, 103), (QS,), 0, BLOCK)
    return (shard_blocks, shard_blocks * BLOCK - shortfall)


def draw_block_count(key, part):
    shard_blocks, filled = shard_loads(key)
    return shard_blocks


def draw_ent_val(key, part):
    shard_blocks, filled = shard_loads(key)
    key = jax.random.fold_in(key, 7)
    uniform_draw = jax.random.uniform(key, (QS, MAXB * BLOCK), jnp.float32, 1.0, 6.0)
    slot_index = jnp.arange(MAXB * BLOCK)[None, :]
    return jnp.where(slot_index < filled[:, None], uniform_draw, jnp.float32(0.0)).astype(jnp.bfloat16)


def plant(entries, stream_key, least, top_value):
    index_at = [jax.random.randint(jax.random.fold_in(stream_key, axis), (), 0, length) for axis, length in enumerate(entries.shape)]
    widest = entries.shape.index(max(entries.shape))
    next_to = index_at[:widest] + [(index_at[widest] + 1) % entries.shape[widest]] + index_at[widest + 1:]
    return entries.at[tuple(index_at)].set(least).at[tuple(next_to)].set(top_value)


def block_levels(rng, dims, split, smallest, top_value):
    factor_of, own = 1.0, jax.random.fold_in(rng, 6)
    for dim, blocks in split:
        steps = jnp.exp(jax.random.uniform(jax.random.fold_in(own, dim), (blocks,), jnp.float32, smallest / len(split), top_value / len(split)))
        factor_of = factor_of * jnp.repeat(steps, dims[dim] // blocks).reshape([-1 if axis == dim else 1 for axis in range(len(dims))])
    return factor_of


def centred(own_key, extent, scale, limit, cuts=(), kind=jnp.bfloat16):
    values = jax.random.normal(own_key, extent, jnp.float32) * scale
    if len(cuts) > 0:
        values = block_levels(own_key, extent, cuts, -0.22, 0.18) * values
    return jnp.clip(values, min=-limit, max=limit).astype(kind)


def setup_inputs(seed: int = 0, part: int = 0) -> dict:
    splits = jax.random.split(jax.random.key(seed), 9)
    own_keys = jax.random.split(jax.random.fold_in(splits[8], part), 9)
    target = centred(own_keys[0], (ROWS, DW), 1.0, 6.0, ((0, 8), (1, 2)))
    dec_w = centred(own_keys[1], (LATENTS, DW), 0.03, 0.4375, ((0, 8), (1, 2)))
    mom_first = centred(own_keys[2], (LATENTS, DW), 0.2, 3.0, ((0, 8), (1, 2)))
    mom_second = jnp.clip(jnp.exp(math.log(0.049804688) - 2.3038113 * jax.random.uniform(own_keys[3], (LATENTS, DW), jnp.float32) ** block_levels(own_keys[3], (LATENTS, DW), ((0, 8), (1, 2)), -0.2, 0.2)), 0.0049743652, 0.049804688).astype(jnp.bfloat16)
    ent_row = plant(jax.random.randint(own_keys[4], (QS, MAXB * BLOCK), 0, ROWS), jax.random.fold_in(own_keys[4], 1), 0, ROWS - 1).astype(jnp.int32)
    ent_lat = plant(jax.random.randint(own_keys[5], (QS, MAXB * BLOCK), 0, LAT_DEV), jax.random.fold_in(own_keys[5], 1), 0, LAT_DEV - 1).astype(jnp.int32)
    ent_val = draw_ent_val(jax.random.fold_in(jax.random.fold_in(splits[8], part), 71), part)
    block_count = draw_block_count(jax.random.fold_in(jax.random.fold_in(splits[8], part), 71), part)
    return dict(target=target, dec_w=dec_w, mom_first=mom_first, mom_second=mom_second, ent_row=ent_row, ent_lat=ent_lat, ent_val=ent_val, block_count=block_count)


beta_one = 0.9
beta_two = 0.999
learn_rate = 0.01
epsilon = 1e-08
correct_one = 0.999973438601112
correct_two = 0.095207852886291

def reference(target, dec_w, mom_first, mom_second, ent_row, ent_lat, ent_val, block_count):
    slot_total = ent_row.shape[1]
    shard_total = ent_row.shape[0]
    slot_index = jnp.arange(slot_total, dtype=jnp.int32)[None, :]
    live = slot_index < block_count[:, None] * BLOCK
    live_values = jnp.where(live, ent_val.astype(jnp.float32), jnp.zeros((), jnp.float32))
    global_lats = (jnp.arange(shard_total, dtype=jnp.int32)[:, None] * LAT_DEV + ent_lat).astype(jnp.int32)
    features = dec_w.shape[1]

    def add_shard(total, item):
        row_ids, lat_ids, scales = item
        picked = dec_w[lat_ids].astype(jnp.float32)
        return (total.at[row_ids].add(scales[:, None] * picked), None)
    rebuilt, _ = lax.scan(add_shard, jnp.zeros((ROWS, features), jnp.float32), (ent_row, global_lats, live_values))
    errors = (rebuilt - target.astype(jnp.float32)).astype(jnp.bfloat16)
    errors_wide = errors.astype(jnp.float32)

    def grad_shard(carry, item):
        row_ids, lat_ids, scales = item
        terms = scales[:, None] * errors_wide[row_ids]
        return (carry, jnp.zeros((LAT_DEV, features), jnp.float32).at[lat_ids].add(terms))
    _, pieces = lax.scan(grad_shard, jnp.zeros((), jnp.float32), (ent_row, ent_lat, live_values))
    gradient = pieces.reshape(shard_total * LAT_DEV, features)
    moment_one = beta_one * mom_first.astype(jnp.float32) + (1.0 - beta_one) * gradient
    moment_two = beta_two * mom_second.astype(jnp.float32) + (1.0 - beta_two) * gradient * gradient
    update = learn_rate * (moment_one / correct_one) / (jnp.sqrt(moment_two / correct_two) + epsilon)
    new_w = (dec_w.astype(jnp.float32) - update).astype(jnp.bfloat16)
    return (new_w, moment_one.astype(jnp.bfloat16), moment_two.astype(jnp.bfloat16))
```

```python
import functools
import jax
import jax.numpy as jnp
from jax import lax
from jax.experimental import pallas as pl
from jax.experimental.pallas import tpu as pltpu
from jax.sharding import PartitionSpec as P

BLOCK = 128
MESH = pl.DeviceIdType.MESH

beta_one = 0.9
beta_two = 0.999
learn_rate = 0.01
epsilon = 1e-08
correct_one = 0.999973438601112
correct_two = 0.095207852886291

CHUNK = 256
SPLIT = 2
LAG_MID = 3
LAG_ERR = 2
LAG_OUTER = 6


def adam_apply(weights, first_in, second_in, gradient):
    moment_one = beta_one * first_in.astype(jnp.float32) + (1.0 - beta_one) * gradient
    moment_two = beta_two * second_in.astype(jnp.float32) + (1.0 - beta_two) * gradient * gradient
    update = (
        learn_rate * (moment_one / correct_one) / (jnp.sqrt(moment_two / correct_two) + epsilon)
    )
    new_weights = (weights.astype(jnp.float32) - update).astype(jnp.bfloat16)
    return (new_weights, moment_one.astype(jnp.bfloat16), moment_two.astype(jnp.bfloat16))


def gradient_kernel(
    n, count_ref, row_ref, lat_ref, val_ref, w_ref, target_ref, g_ref,
    spread, pick, codes, part, own, err, sib_out, sib_in, in_out, up_in, mid_in,
    sib_s, sib_r, in_s, up_r, mid_r, out_s, out_r, err_s, err_r,
):
    z, c = lax.axis_index("lat"), lax.axis_index("sub")
    units, half, _ = own.shape
    unit = 2 * half
    share = target_ref.shape[0]
    slots = row_ref.shape[1]
    latents = w_ref.shape[0]
    side = z // (n // 2)
    inner, outer = z + 1 - 2 * side, z - 1 + 2 * side
    depth = z * (1 - side) + (n - 1 - z) * side
    is_end, is_mid = depth == 0, depth == n // 2 - 1
    not_end, not_mid = depth > 0, depth < n // 2 - 1
    sib_id, inner_id, outer_id = {"sub": 1 - c}, {"lat": inner}, {"lat": outer}

    barrier = pltpu.get_barrier_semaphore()
    pl.semaphore_signal(barrier, inc=1, device_id=sib_id, device_id_type=MESH)
    pl.semaphore_signal(barrier, inc=1, device_id=inner_id, device_id_type=MESH)

    @pl.when(not_end)
    def _():
        pl.semaphore_signal(barrier, inc=1, device_id=outer_id, device_id_type=MESH)
        pl.semaphore_wait(barrier, 3)

    @pl.when(is_end)
    def _():
        pl.semaphore_wait(barrier, 2)

    def rows_of(u, which):
        return pl.ds(pl.multiple_of(u * unit + which * half, 16), half)

    def sib_copy(u):
        return pltpu.make_async_remote_copy(
            src_ref=sib_out.at[u], dst_ref=sib_in.at[u], send_sem=sib_s.at[u],
            recv_sem=sib_r.at[u], device_id=sib_id, device_id_type=MESH)

    def up_copy(u):
        return pltpu.make_async_remote_copy(
            src_ref=in_out.at[u], dst_ref=up_in.at[u], send_sem=in_s.at[u],
            recv_sem=up_r.at[u], device_id=inner_id, device_id_type=MESH)

    def mid_copy(u):
        return pltpu.make_async_remote_copy(
            src_ref=in_out.at[u], dst_ref=mid_in.at[u], send_sem=in_s.at[u],
            recv_sem=mid_r.at[u], device_id=inner_id, device_id_type=MESH)

    def out_copy(u):
        return pltpu.make_async_remote_copy(
            src_ref=err.at[rows_of(u, c)], dst_ref=err.at[rows_of(u, c)], send_sem=out_s.at[u],
            recv_sem=out_r.at[u], device_id=outer_id, device_id_type=MESH)

    def err_copy(u, which):
        return pltpu.make_async_remote_copy(
            src_ref=err.at[rows_of(u, which)], dst_ref=err.at[rows_of(u, which)],
            send_sem=err_s.at[u], recv_sem=err_r.at[u], device_id=sib_id, device_id_type=MESH)

    live = lax.broadcasted_iota(jnp.int32, (1, slots), 1) < count_ref[0] * BLOCK
    values = jnp.where(live, val_ref[...].astype(jnp.float32), 0.0)

    @pl.loop(0, latents // BLOCK)
    def _(k):
        at = lax.broadcasted_iota(jnp.int32, (BLOCK, slots), 0) + k * BLOCK
        spread[pl.ds(pl.multiple_of(k * BLOCK, BLOCK), BLOCK), :] = jnp.where(
            at == lat_ref[...], values, 0.0
        ).astype(jnp.bfloat16)

    g_ref[...] = jnp.zeros_like(g_ref)

    def compute(b):
        rows = pl.ds(pl.multiple_of(b * CHUNK, CHUNK), CHUNK)
        at = lax.broadcasted_iota(jnp.int32, (CHUNK, slots), 0) + b * CHUNK
        pick[...] = jnp.where(at == row_ref[...], 1.0, 0.0).astype(jnp.bfloat16)
        codes[rows, :] = lax.dot_general(
            pick[...], spread[...], (((1,), (1,)), ((), ())), preferred_element_type=jnp.float32
        ).astype(jnp.bfloat16)
        part[...] = jnp.dot(codes[rows, :], w_ref[...], preferred_element_type=jnp.float32)
        first = (z * 2 + c) * share

        @pl.when(first // CHUNK == b)
        def _():
            at_own = pl.ds(pl.multiple_of(lax.rem(first, CHUNK), 16), share)
            part[at_own, :] = part[at_own, :] - target_ref[...].astype(jnp.float32)

        for j in range(SPLIT):
            u = b * SPLIT + j
            theirs = pl.ds(pl.multiple_of(j * unit + (1 - c) * half, 16), half)
            mine = pl.ds(pl.multiple_of(j * unit + c * half, 16), half)
            sib_out[u] = part[theirs, :].astype(jnp.bfloat16)
            sib_copy(u).start()
            own[u] = part[mine, :]

    def relay(u):
        sib_copy(u).wait_recv()
        own[u] = own[u] + sib_in[u].astype(jnp.float32)

        @pl.when(not_end)
        def _():
            up_copy(u).wait_recv()
            own[u] = own[u] + up_in[u].astype(jnp.float32)

        in_out[u] = own[u].astype(jnp.bfloat16)

        @pl.when(is_mid)
        def _():
            mid_copy(u).start()

        @pl.when(not_mid)
        def _():
            up_copy(u).start()

    def errors(u):
        @pl.when(is_mid)
        def _():
            mid_copy(u).wait_recv()
            err[rows_of(u, c), :] = (own[u] + mid_in[u].astype(jnp.float32)).astype(jnp.bfloat16)

        @pl.when(not_mid)
        def _():
            out_copy(u).wait_recv()

        @pl.when(not_end)
        def _():
            out_copy(u).start()

        err_copy(u, c).start()

    def collect(u):
        err_copy(u, 1 - c).wait_recv()
        rows = pl.ds(pl.multiple_of(u * unit, unit), unit)
        g_ref[...] += lax.dot_general(
            codes[rows, :], err[rows, :], (((0,), (0,)), ((), ())),
            preferred_element_type=jnp.float32,
        )

    end = lax.max(1 - depth, 0)
    lag_in = (1 - end) * LAG_MID
    lag_err = lag_in + (1 - end) * LAG_ERR + end * LAG_OUTER
    lag_all = lag_err + 1

    @pl.loop(0, units + max(LAG_OUTER, LAG_MID + LAG_ERR) + 1)
    def _(t):
        @pl.when((t < units) & (lax.rem(t, SPLIT) == 0))
        def _():
            compute(t // SPLIT)

        @pl.when((t >= lag_in) & (t < units + lag_in))
        def _():
            relay(t - lag_in)

        @pl.when((t >= lag_err) & (t < units + lag_err))
        def _():
            errors(t - lag_err)

        @pl.when((t >= lag_all) & (t < units + lag_all))
        def _():
            collect(t - lag_all)

    @pl.loop(0, units)
    def _(u):
        sib_copy(u).wait_send()
        up_copy(u).wait_send()
        err_copy(u, c).wait_send()

        @pl.when(not_end)
        def _():
            out_copy(u).wait_send()


def on_device(n, target, dec_w, mom_first, mom_second, ent_row, ent_lat, ent_val, block_count):
    latents, features = dec_w.shape
    slots = ent_row.shape[1]
    rows = target.shape[0] * n * 2
    units = rows // CHUNK * SPLIT
    half = CHUNK // SPLIT // 2
    vmem = pl.BlockSpec(memory_space=pltpu.VMEM)
    block = (units, half, features)
    gradient = pl.pallas_call(
        functools.partial(gradient_kernel, n),
        out_shape=jax.ShapeDtypeStruct((latents, features), jnp.float32),
        in_specs=[pl.BlockSpec(memory_space=pltpu.SMEM)] + [vmem] * 5,
        out_specs=vmem,
        scratch_shapes=[
            pltpu.VMEM((latents, slots), jnp.bfloat16),
            pltpu.VMEM((CHUNK, slots), jnp.bfloat16),
            pltpu.VMEM((rows, latents), jnp.bfloat16),
            pltpu.VMEM((CHUNK, features), jnp.float32),
            pltpu.VMEM(block, jnp.float32),
            pltpu.VMEM((rows, features), jnp.bfloat16),
        ]
        + [pltpu.VMEM(block, jnp.bfloat16)] * 5
        + [pltpu.SemaphoreType.DMA((units,))] * 9,
        compiler_params=pltpu.CompilerParams(
            collective_id=0, has_side_effects=True, vmem_limit_bytes=40 * 2**20
        ),
        cost_estimate=pl.CostEstimate(
            flops=2 * rows * latents * (slots + 2 * features),
            bytes_accessed=6 * latents * features, transcendentals=0,
        ),
    )(block_count, ent_row, ent_lat, ent_val, dec_w, target)
    return adam_apply(dec_w, mom_first, mom_second, gradient)


def solution(mesh):
    shard = P(("groups", "lat", "sub"), "row")
    entries = P(("groups", "lat", "sub"), None)
    return jax.shard_map(
        functools.partial(on_device, mesh.shape["lat"]), mesh=mesh,
        in_specs=(shard, shard, shard, shard, entries, entries, entries, P(("groups", "lat", "sub"))),
        out_specs=(shard, shard, shard), check_vma=False,
    )
```

```python
import functools
import jax
import jax.numpy as jnp
from jax import lax
from jax.experimental import pallas as pl
from jax.experimental.pallas import tpu as pltpu
from jax.sharding import PartitionSpec as P

BLOCK = 128
MESH = pl.DeviceIdType.MESH

beta_one = 0.9
beta_two = 0.999
learn_rate = 0.01
epsilon = 1e-08
correct_one = 0.999973438601112
correct_two = 0.095207852886291

TILE = 128
CHUNK = 256
SPLIT = 2
LAG_MID = 3
LAG_ERR = 2
LAG_OUTER = 6


def adam_kernel(g_ref, w_ref, first_ref, second_ref, w_out, first_out, second_out,
                w_tile, first_tile, second_tile, sems):
    tiles = g_ref.shape[0] // TILE

    def copies(k):
        rows = pl.ds(pl.multiple_of(k * TILE, TILE), TILE)
        return [
            pltpu.make_async_copy(tile.at[rows], out.at[rows], sems.at[i, k])
            for i, (tile, out) in enumerate(
                ((w_tile, w_out), (first_tile, first_out), (second_tile, second_out)))
        ]

    @pl.loop(0, tiles)
    def _(k):
        rows = pl.ds(pl.multiple_of(k * TILE, TILE), TILE)
        gradient = g_ref[rows, :]
        moment_one = (
            beta_one * first_ref[rows, :].astype(jnp.float32) + (1.0 - beta_one) * gradient
        )
        moment_two = beta_two * second_ref[rows, :].astype(jnp.float32) + (
            ((1.0 - beta_two) * gradient) * gradient
        )
        root = lax.rsqrt(moment_two) * moment_two * (1.0 / correct_two) ** 0.5 + epsilon
        update = (learn_rate / correct_one) * moment_one * pl.reciprocal(root, approx=True)
        w_tile[rows, :] = (w_ref[rows, :].astype(jnp.float32) - update).astype(jnp.bfloat16)
        first_tile[rows, :] = moment_one.astype(jnp.bfloat16)
        second_tile[rows, :] = moment_two.astype(jnp.bfloat16)
        for copy in copies(k):
            copy.start()

    @pl.loop(0, tiles)
    def _(k):
        for copy in copies(k):
            copy.wait()


def gradient_kernel(
    n, count_ref, row_hbm, lat_hbm, val_hbm, w_hbm, target_hbm, g_ref,
    row_ref, lat_ref, val_ref, w_ref, target_ref, load, spread, pick, codes, part, own, err, sib_out, sib_in, in_out, up_in, mid_in,
    sib_s, sib_r, in_s, up_r, mid_r, out_s, out_r, err_s, err_r,
):
    z, c = lax.axis_index("lat"), lax.axis_index("sub")
    units, half, _ = own.shape
    unit = 2 * half
    share = target_ref.shape[0]
    slots = row_ref.shape[1]
    latents = w_ref.shape[0]
    side = z // (n // 2)
    inner, outer = z + 1 - 2 * side, z - 1 + 2 * side
    depth = z * (1 - side) + (n - 1 - z) * side
    is_end, is_mid = depth == 0, depth == n // 2 - 1
    not_end, not_mid = depth > 0, depth < n // 2 - 1
    sib_id, inner_id, outer_id = {"sub": 1 - c}, {"lat": inner}, {"lat": outer}

    loads = [
        pltpu.make_async_copy(src, dst, load.at[i])
        for i, (src, dst) in enumerate((
            (row_hbm, row_ref), (lat_hbm, lat_ref), (val_hbm, val_ref), (w_hbm, w_ref),
            (target_hbm, target_ref)))
    ]
    for copy in loads:
        copy.start()

    barrier = pltpu.get_barrier_semaphore()
    pl.semaphore_signal(barrier, inc=1, device_id=sib_id, device_id_type=MESH)
    pl.semaphore_signal(barrier, inc=1, device_id=inner_id, device_id_type=MESH)

    @pl.when(not_end)
    def _():
        pl.semaphore_signal(barrier, inc=1, device_id=outer_id, device_id_type=MESH)

    def wait_partners():
        @pl.when(not_end)
        def _():
            pl.semaphore_wait(barrier, 3)

        @pl.when(is_end)
        def _():
            pl.semaphore_wait(barrier, 2)

    def rows_of(u, which):
        return pl.ds(pl.multiple_of(u * unit + which * half, 16), half)

    def sib_copy(u):
        return pltpu.make_async_remote_copy(
            src_ref=sib_out.at[u], dst_ref=sib_in.at[u], send_sem=sib_s.at[u],
            recv_sem=sib_r.at[u], device_id=sib_id, device_id_type=MESH)

    def up_copy(u):
        return pltpu.make_async_remote_copy(
            src_ref=in_out.at[u], dst_ref=up_in.at[u], send_sem=in_s.at[u],
            recv_sem=up_r.at[u], device_id=inner_id, device_id_type=MESH)

    def mid_copy(u):
        return pltpu.make_async_remote_copy(
            src_ref=in_out.at[u], dst_ref=mid_in.at[u], send_sem=in_s.at[u],
            recv_sem=mid_r.at[u], device_id=inner_id, device_id_type=MESH)

    def out_copy(u):
        return pltpu.make_async_remote_copy(
            src_ref=err.at[rows_of(u, c)], dst_ref=err.at[rows_of(u, c)], send_sem=out_s.at[u],
            recv_sem=out_r.at[u], device_id=outer_id, device_id_type=MESH)

    def err_copy(u, which):
        return pltpu.make_async_remote_copy(
            src_ref=err.at[rows_of(u, which)], dst_ref=err.at[rows_of(u, which)],
            send_sem=err_s.at[u], recv_sem=err_r.at[u], device_id=sib_id, device_id_type=MESH)

    for copy in loads[:3]:
        copy.wait()

    live = lax.broadcasted_iota(jnp.int32, (1, slots), 1) < count_ref[0] * BLOCK
    values = jnp.where(live, val_ref[...].astype(jnp.float32), 0.0)

    @pl.loop(0, latents // BLOCK)
    def _(k):
        at = lax.broadcasted_iota(jnp.int32, (BLOCK, slots), 0) + k * BLOCK
        spread[pl.ds(pl.multiple_of(k * BLOCK, BLOCK), BLOCK), :] = jnp.where(
            at == lat_ref[...], values, 0.0
        ).astype(jnp.bfloat16)

    def compute(b):
        rows = pl.ds(pl.multiple_of(b * CHUNK, CHUNK), CHUNK)
        at = lax.broadcasted_iota(jnp.int32, (CHUNK, slots), 0) + b * CHUNK
        pick[...] = jnp.where(at == row_ref[...], 1.0, 0.0).astype(jnp.bfloat16)
        codes[rows, :] = lax.dot_general(
            pick[...], spread[...], (((1,), (1,)), ((), ())), preferred_element_type=jnp.float32
        ).astype(jnp.bfloat16)

        @pl.when(b == 0)
        def _():
            for copy in loads[3:]:
                copy.wait()

        part[...] = jnp.dot(codes[rows, :], w_ref[...], preferred_element_type=jnp.float32)
        first = (z * 2 + c) * share

        @pl.when(first // CHUNK == b)
        def _():
            at_own = pl.ds(pl.multiple_of(lax.rem(first, CHUNK), 16), share)
            part[at_own, :] = part[at_own, :] - target_ref[...].astype(jnp.float32)

        @pl.when(b == 0)
        def _():
            wait_partners()

        for j in range(SPLIT):
            u = b * SPLIT + j
            theirs = pl.ds(pl.multiple_of(j * unit + (1 - c) * half, 16), half)
            mine = pl.ds(pl.multiple_of(j * unit + c * half, 16), half)
            sib_out[u] = part[theirs, :].astype(jnp.bfloat16)
            sib_copy(u).start()
            own[u] = part[mine, :]

    def relay(u):
        sib_copy(u).wait_recv()
        own[u] = own[u] + sib_in[u].astype(jnp.float32)

        @pl.when(not_end)
        def _():
            up_copy(u).wait_recv()
            own[u] = own[u] + up_in[u].astype(jnp.float32)

        in_out[u] = own[u].astype(jnp.bfloat16)

        @pl.when(is_mid)
        def _():
            mid_copy(u).start()

        @pl.when(not_mid)
        def _():
            up_copy(u).start()

    def errors(u):
        @pl.when(is_mid)
        def _():
            mid_copy(u).wait_recv()
            err[rows_of(u, c), :] = (own[u] + mid_in[u].astype(jnp.float32)).astype(jnp.bfloat16)

        @pl.when(not_mid)
        def _():
            out_copy(u).wait_recv()

        @pl.when(not_end)
        def _():
            out_copy(u).start()

        err_copy(u, c).start()

    def collect(u):
        err_copy(u, 1 - c).wait_recv()

        @pl.when(lax.rem(u, SPLIT) == SPLIT - 1)
        def _():
            rows = pl.ds(pl.multiple_of(u // SPLIT * CHUNK, CHUNK), CHUNK)
            g_ref[...] += lax.dot_general(
                codes[rows, :], err[rows, :], (((0,), (0,)), ((), ())),
                preferred_element_type=jnp.float32,
            )

    end = lax.max(1 - depth, 0)
    lag_in = (1 - end) * LAG_MID
    lag_err = lag_in + (1 - end) * LAG_ERR + end * LAG_OUTER
    lag_all = lag_err + 1

    @pl.loop(0, units + max(LAG_OUTER, LAG_MID + LAG_ERR) + 1)
    def _(t):
        @pl.when((t < units) & (lax.rem(t, SPLIT) == 0))
        def _():
            compute(t // SPLIT)

        @pl.when((t >= lag_in) & (t < units + lag_in))
        def _():
            relay(t - lag_in)

        @pl.when(t == 0)
        def _():
            g_ref[...] = jnp.zeros_like(g_ref)

        @pl.when((t >= lag_err) & (t < units + lag_err))
        def _():
            errors(t - lag_err)

        @pl.when((t >= lag_all) & (t < units + lag_all))
        def _():
            collect(t - lag_all)

    @pl.loop(0, units)
    def _(u):
        sib_copy(u).wait_send()
        up_copy(u).wait_send()
        err_copy(u, c).wait_send()

        @pl.when(not_end)
        def _():
            out_copy(u).wait_send()


def on_device(n, target, dec_w, mom_first, mom_second, ent_row, ent_lat, ent_val, block_count):
    latents, features = dec_w.shape
    slots = ent_row.shape[1]
    rows = target.shape[0] * n * 2
    units = rows // CHUNK * SPLIT
    half = CHUNK // SPLIT // 2
    ent_row, ent_lat, ent_val, w_far, target = [
        pltpu.with_memory_space_constraint(x, pltpu.HBM)
        for x in (ent_row, ent_lat, ent_val, dec_w, target)
    ]
    hbm = pl.BlockSpec(memory_space=pltpu.HBM)
    vmem = pl.BlockSpec(memory_space=pltpu.VMEM)
    block = (units, half, features)
    gradient = pl.pallas_call(
        functools.partial(gradient_kernel, n),
        out_shape=jax.ShapeDtypeStruct((latents, features), jnp.float32),
        in_specs=[pl.BlockSpec(memory_space=pltpu.SMEM)] + [hbm] * 5,
        out_specs=vmem,
        scratch_shapes=[
            pltpu.VMEM(ent_row.shape, jnp.int32),
            pltpu.VMEM(ent_lat.shape, jnp.int32),
            pltpu.VMEM(ent_val.shape, jnp.bfloat16),
            pltpu.VMEM(dec_w.shape, jnp.bfloat16),
            pltpu.VMEM(target.shape, jnp.bfloat16),
            pltpu.SemaphoreType.DMA((5,)),
            pltpu.VMEM((latents, slots), jnp.bfloat16),
            pltpu.VMEM((CHUNK, slots), jnp.bfloat16),
            pltpu.VMEM((rows, latents), jnp.bfloat16),
            pltpu.VMEM((CHUNK, features), jnp.float32),
            pltpu.VMEM(block, jnp.float32),
            pltpu.VMEM((rows, features), jnp.bfloat16),
        ]
        + [pltpu.VMEM(block, jnp.bfloat16)] * 5
        + [pltpu.SemaphoreType.DMA((units,))] * 9,
        compiler_params=pltpu.CompilerParams(
            collective_id=0, has_side_effects=True, vmem_limit_bytes=40 * 2**20
        ),
        cost_estimate=pl.CostEstimate(
            flops=2 * rows * latents * (slots + 2 * features),
            bytes_accessed=6 * latents * features, transcendentals=0,
        ),
    )(block_count, ent_row, ent_lat, ent_val, w_far, target)
    return pl.pallas_call(
        adam_kernel,
        out_shape=[jax.ShapeDtypeStruct((latents, features), jnp.bfloat16)] * 3,
        in_specs=[vmem] * 4,
        out_specs=[hbm] * 3,
        scratch_shapes=[pltpu.VMEM((latents, features), jnp.bfloat16)] * 3
        + [pltpu.SemaphoreType.DMA((3, latents // TILE))],
        compiler_params=pltpu.CompilerParams(vmem_limit_bytes=12 * 2**20),
        cost_estimate=pl.CostEstimate(
            flops=20 * latents * features, bytes_accessed=16 * latents * features,
            transcendentals=2 * latents * features,
        ),
    )(gradient, dec_w, mom_first, mom_second)


def solution(mesh):
    shard = P(("groups", "lat", "sub"), "row")
    entries = P(("groups", "lat", "sub"), None)
    return jax.shard_map(
        functools.partial(on_device, mesh.shape["lat"]), mesh=mesh,
        in_specs=(shard, shard, shard, shard, entries, entries, entries, P(("groups", "lat", "sub"))),
        out_specs=(shard, shard, shard), check_vma=False,
    )
```

```python
import functools
import jax
import jax.numpy as jnp
from jax import lax
from jax.experimental import pallas as pl
from jax.experimental.pallas import tpu as pltpu
from jax.sharding import PartitionSpec as P

BLOCK = 128
MESH = pl.DeviceIdType.MESH

beta_one = 0.9
beta_two = 0.999
learn_rate = 0.01
epsilon = 1e-08
correct_one = 0.999973438601112
correct_two = 0.095207852886291

TILE = 128
CHUNK = 256
SPLIT = 2
LAG_MID = 3
LAG_ERR = 2
LAG_OUTER = 6


def adam_kernel(g_ref, w_ref, first_ref, second_ref, w_out, first_out, second_out,
                w_tile, first_tile, second_tile, sems):
    tiles = g_ref.shape[0] // TILE

    def copies(k):
        rows = pl.ds(pl.multiple_of(k * TILE, TILE), TILE)
        return [
            pltpu.make_async_copy(tile.at[rows], out.at[rows], sems.at[i, k])
            for i, (tile, out) in enumerate(
                ((w_tile, w_out), (first_tile, first_out), (second_tile, second_out)))
        ]

    @pl.loop(0, tiles)
    def _(k):
        rows = pl.ds(pl.multiple_of(k * TILE, TILE), TILE)
        gradient = g_ref[rows, :]
        moment_one = (
            beta_one * first_ref[rows, :].astype(jnp.float32) + (1.0 - beta_one) * gradient
        )
        moment_two = beta_two * second_ref[rows, :].astype(jnp.float32) + (
            ((1.0 - beta_two) * gradient) * gradient
        )
        root = lax.rsqrt(moment_two) * moment_two * (1.0 / correct_two) ** 0.5 + epsilon
        update = (learn_rate / correct_one) * moment_one * pl.reciprocal(root, approx=True)
        w_tile[rows, :] = (w_ref[rows, :].astype(jnp.float32) - update).astype(jnp.bfloat16)
        first_tile[rows, :] = moment_one.astype(jnp.bfloat16)
        second_tile[rows, :] = moment_two.astype(jnp.bfloat16)
        for copy in copies(k):
            copy.start()

    @pl.loop(0, tiles)
    def _(k):
        for copy in copies(k):
            copy.wait()


def gradient_kernel(
    n, count_ref, row_hbm, lat_hbm, val_hbm, w_hbm, target_hbm, g_ref,
    row_ref, lat_ref, val_ref, w_ref, target_ref, load, spread, pick, codes, part, own, err, sib_out, sib_in, in_out, up_in, mid_in,
    sib_s, sib_r, in_s, up_r, mid_r, out_s, out_r, err_s, err_r,
):
    z, c = lax.axis_index("lat"), lax.axis_index("sub")
    units, half, _ = own.shape
    unit = 2 * half
    share = target_ref.shape[0]
    slots = row_ref.shape[1]
    latents = w_ref.shape[0]
    side = z // (n // 2)
    inner, outer = z + 1 - 2 * side, z - 1 + 2 * side
    depth = z * (1 - side) + (n - 1 - z) * side
    is_end, is_mid = depth == 0, depth == n // 2 - 1
    not_end, not_mid = depth > 0, depth < n // 2 - 1
    sib_id, inner_id, outer_id = {"sub": 1 - c}, {"lat": inner}, {"lat": outer}

    loads = [
        pltpu.make_async_copy(src, dst, load.at[i])
        for i, (src, dst) in enumerate((
            (row_hbm, row_ref), (lat_hbm, lat_ref), (val_hbm, val_ref), (w_hbm, w_ref),
            (target_hbm, target_ref)))
    ]
    for copy in loads:
        copy.start()

    barrier = pltpu.get_barrier_semaphore()
    pl.semaphore_signal(barrier, inc=1, device_id=sib_id, device_id_type=MESH)
    pl.semaphore_signal(barrier, inc=1, device_id=inner_id, device_id_type=MESH)

    @pl.when(not_end)
    def _():
        pl.semaphore_signal(barrier, inc=1, device_id=outer_id, device_id_type=MESH)

    def wait_partners():
        @pl.when(not_end)
        def _():
            pl.semaphore_wait(barrier, 3)

        @pl.when(is_end)
        def _():
            pl.semaphore_wait(barrier, 2)

    def rows_of(u, which):
        return pl.ds(pl.multiple_of(u * unit + which * half, 16), half)

    def sib_copy(u):
        return pltpu.make_async_remote_copy(
            src_ref=sib_out.at[u], dst_ref=sib_in.at[u], send_sem=sib_s.at[u],
            recv_sem=sib_r.at[u], device_id=sib_id, device_id_type=MESH)

    def up_copy(u):
        return pltpu.make_async_remote_copy(
            src_ref=in_out.at[u], dst_ref=up_in.at[u], send_sem=in_s.at[u],
            recv_sem=up_r.at[u], device_id=inner_id, device_id_type=MESH)

    def mid_copy(u):
        return pltpu.make_async_remote_copy(
            src_ref=in_out.at[u], dst_ref=mid_in.at[u], send_sem=in_s.at[u],
            recv_sem=mid_r.at[u], device_id=inner_id, device_id_type=MESH)

    def out_copy(u):
        return pltpu.make_async_remote_copy(
            src_ref=err.at[rows_of(u, c)], dst_ref=err.at[rows_of(u, c)], send_sem=out_s.at[u],
            recv_sem=out_r.at[u], device_id=outer_id, device_id_type=MESH)

    def err_copy(u, which):
        return pltpu.make_async_remote_copy(
            src_ref=err.at[rows_of(u, which)], dst_ref=err.at[rows_of(u, which)],
            send_sem=err_s.at[u], recv_sem=err_r.at[u], device_id=sib_id, device_id_type=MESH)

    for copy in loads[:3]:
        copy.wait()

    live = lax.broadcasted_iota(jnp.int32, (1, slots), 1) < count_ref[0] * BLOCK
    values = jnp.where(live, val_ref[...].astype(jnp.float32), 0.0)

    @pl.loop(0, latents // BLOCK)
    def _(k):
        at = lax.broadcasted_iota(jnp.int32, (BLOCK, slots), 0) + k * BLOCK
        spread[pl.ds(pl.multiple_of(k * BLOCK, BLOCK), BLOCK), :] = jnp.where(
            at == lat_ref[...], values, 0.0
        ).astype(jnp.bfloat16)

    def compute(b):
        rows = pl.ds(pl.multiple_of(b * CHUNK, CHUNK), CHUNK)
        at = lax.broadcasted_iota(jnp.int32, (CHUNK, slots), 0) + b * CHUNK
        pick[...] = jnp.where(at == row_ref[...], 1.0, 0.0).astype(jnp.bfloat16)
        codes[rows, :] = lax.dot_general(
            pick[...], spread[...], (((1,), (1,)), ((), ())), preferred_element_type=jnp.float32
        ).astype(jnp.bfloat16)

        @pl.when(b == 0)
        def _():
            for copy in loads[3:]:
                copy.wait()

        part[...] = jnp.dot(codes[rows, :], w_ref[...], preferred_element_type=jnp.float32)
        first = (z * 2 + c) * share

        @pl.when(first // CHUNK == b)
        def _():
            at_own = pl.ds(pl.multiple_of(lax.rem(first, CHUNK), 16), share)
            part[at_own, :] = part[at_own, :] - target_ref[...].astype(jnp.float32)

        for j in range(SPLIT):
            u = b * SPLIT + j
            theirs = pl.ds(pl.multiple_of(j * unit + (1 - c) * half, 16), half)
            mine = pl.ds(pl.multiple_of(j * unit + c * half, 16), half)
            sib_out[u] = part[theirs, :].astype(jnp.bfloat16)
            sib_copy(u).start()
            own[u] = part[mine, :]

    def relay(u):
        sib_copy(u).wait_recv()
        own[u] = own[u] + sib_in[u].astype(jnp.float32)

        @pl.when(not_end)
        def _():
            up_copy(u).wait_recv()
            own[u] = own[u] + up_in[u].astype(jnp.float32)

        in_out[u] = own[u].astype(jnp.bfloat16)

        @pl.when(is_mid)
        def _():
            mid_copy(u).start()

        @pl.when(not_mid)
        def _():
            up_copy(u).start()

    def errors(u):
        @pl.when(is_mid)
        def _():
            mid_copy(u).wait_recv()
            err[rows_of(u, c), :] = (own[u] + mid_in[u].astype(jnp.float32)).astype(jnp.bfloat16)

        @pl.when(not_mid)
        def _():
            out_copy(u).wait_recv()

        @pl.when(not_end)
        def _():
            out_copy(u).start()

        err_copy(u, c).start()

    def collect(u):
        err_copy(u, 1 - c).wait_recv()

        @pl.when(lax.rem(u, SPLIT) == SPLIT - 1)
        def _():
            rows = pl.ds(pl.multiple_of(u // SPLIT * CHUNK, CHUNK), CHUNK)
            g_ref[...] += lax.dot_general(
                codes[rows, :], err[rows, :], (((0,), (0,)), ((), ())),
                preferred_element_type=jnp.float32,
            )

    end = lax.max(1 - depth, 0)
    lag_in = (1 - end) * LAG_MID + end
    lag_err = lag_in + (1 - end) * LAG_ERR + end * LAG_OUTER
    lag_all = lag_err + 1

    wait_partners()

    @pl.loop(0, units + max(LAG_OUTER + 1, LAG_MID + LAG_ERR) + 1)
    def _(t):
        @pl.when((t >= lag_in) & (t < units + lag_in))
        def _():
            relay(t - lag_in)

        @pl.when(t == 0)
        def _():
            g_ref[...] = jnp.zeros_like(g_ref)

        @pl.when((t >= lag_err) & (t < units + lag_err))
        def _():
            errors(t - lag_err)

        @pl.when((t < units) & (lax.rem(t, SPLIT) == 0))
        def _():
            compute(t // SPLIT)

        @pl.when((t >= lag_all) & (t < units + lag_all))
        def _():
            collect(t - lag_all)

    @pl.loop(0, units)
    def _(u):
        sib_copy(u).wait_send()
        up_copy(u).wait_send()
        err_copy(u, c).wait_send()

        @pl.when(not_end)
        def _():
            out_copy(u).wait_send()


def on_device(n, target, dec_w, mom_first, mom_second, ent_row, ent_lat, ent_val, block_count):
    latents, features = dec_w.shape
    slots = ent_row.shape[1]
    rows = target.shape[0] * n * 2
    units = rows // CHUNK * SPLIT
    half = CHUNK // SPLIT // 2
    ent_row, ent_lat, ent_val, w_far, target = [
        pltpu.with_memory_space_constraint(x, pltpu.HBM)
        for x in (ent_row, ent_lat, ent_val, dec_w, target)
    ]
    hbm = pl.BlockSpec(memory_space=pltpu.HBM)
    vmem = pl.BlockSpec(memory_space=pltpu.VMEM)
    block = (units, half, features)
    gradient = pl.pallas_call(
        functools.partial(gradient_kernel, n),
        out_shape=jax.ShapeDtypeStruct((latents, features), jnp.float32),
        in_specs=[pl.BlockSpec(memory_space=pltpu.SMEM)] + [hbm] * 5,
        out_specs=vmem,
        scratch_shapes=[
            pltpu.VMEM(ent_row.shape, jnp.int32),
            pltpu.VMEM(ent_lat.shape, jnp.int32),
            pltpu.VMEM(ent_val.shape, jnp.bfloat16),
            pltpu.VMEM(dec_w.shape, jnp.bfloat16),
            pltpu.VMEM(target.shape, jnp.bfloat16),
            pltpu.SemaphoreType.DMA((5,)),
            pltpu.VMEM((latents, slots), jnp.bfloat16),
            pltpu.VMEM((CHUNK, slots), jnp.bfloat16),
            pltpu.VMEM((rows, latents), jnp.bfloat16),
            pltpu.VMEM((CHUNK, features), jnp.float32),
            pltpu.VMEM(block, jnp.float32),
            pltpu.VMEM((rows, features), jnp.bfloat16),
        ]
        + [pltpu.VMEM(block, jnp.bfloat16)] * 5
        + [pltpu.SemaphoreType.DMA((units,))] * 9,
        compiler_params=pltpu.CompilerParams(
            collective_id=0, has_side_effects=True, vmem_limit_bytes=40 * 2**20
        ),
        cost_estimate=pl.CostEstimate(
            flops=2 * rows * latents * (slots + 2 * features),
            bytes_accessed=6 * latents * features, transcendentals=0,
        ),
    )(block_count, ent_row, ent_lat, ent_val, w_far, target)
    return pl.pallas_call(
        adam_kernel,
        out_shape=[jax.ShapeDtypeStruct((latents, features), jnp.bfloat16)] * 3,
        in_specs=[vmem] * 4,
        out_specs=[hbm] * 3,
        scratch_shapes=[pltpu.VMEM((latents, features), jnp.bfloat16)] * 3
        + [pltpu.SemaphoreType.DMA((3, latents // TILE))],
        compiler_params=pltpu.CompilerParams(vmem_limit_bytes=12 * 2**20),
        cost_estimate=pl.CostEstimate(
            flops=20 * latents * features, bytes_accessed=16 * latents * features,
            transcendentals=2 * latents * features,
        ),
    )(gradient, dec_w, mom_first, mom_second)


def solution(mesh):
    shard = P(("groups", "lat", "sub"), "row")
    entries = P(("groups", "lat", "sub"), None)
    return jax.shard_map(
        functools.partial(on_device, mesh.shape["lat"]), mesh=mesh,
        in_specs=(shard, shard, shard, shard, entries, entries, entries, P(("groups", "lat", "sub"))),
        out_specs=(shard, shard, shard), check_vma=False,
    )
```
